256 devices in a mesh: row: 16 (over x, z_lo), col: 16 (over y, z_hi, core).
Axes of the slice: x: 4, y: 4, z: 8 (z_hi: 2, z_lo: 4; z = z_hi * 4 + z_lo), core: 2. Of those that a mesh axis runs over, the one named last changes fastest.
Arguments:
- tokens: bfloat16 [512, 16384], P('col', 'row'), may hold values from -6 to 6
- gate_codes: bfloat16 [16384, 28672], P('row', 'col'), may hold values from -0.046875 to 0.046875
- gate_scale: float32 [64, 112], P('row', 'col'), may hold values from 0.5 to 5
- up_codes: bfloat16 [16384, 28672], P('row', 'col'), may hold values from -0.046875 to 0.046875
- up_scale: float32 [64, 112], P('row', 'col'), may hold values from 0.5 to 5
- gate_keep: int32 [64, 112], P('row', 'col'), may hold values from 0 to 1, as said below
- down_codes: bfloat16 [28672, 16384], P('col', 'row'), may hold values from -0.03125 to 0.03125
- down_scale: float32 [112, 64], P('col', 'row'), may hold values from 0.5 to 5
- down_keep: int32 [112, 64], P('col', 'row'), may hold values from 0 to 1, as said below
Outputs:
- mixed: bfloat16 [512, 16384], P('col', 'row')
The draws below stay inside these ranges and needn't reach their ends.
Inputs may be any that keep to these rules, and one draw needn't show every extreme that they name: `gate_keep`: 1 keeps a tile and 0 drops it. One device's block of tiles keeps at most 19, and some block keeps exactly that many in every draw; two blocks at the same col index whose row indices differ by half the row axis keep exactly 22 tiles together. `down_keep`: 1 keeps a tile and 0 drops it.
All inputs are finite; a program needn't handle non-finite values.
Results may differ from the reference program's by a relative error of at most 0.0071.
Values may be sent and summed in bfloat16 or wider, within the bound.
A program may use at most 128 MiB of HBM per device.

```python
import math
import jax
import jax.numpy as jnp
from jax import lax

D = 16384
FF = 28672
TILE = 256
TOKENS = 512
ROW_TILES = 4
COL_TILES = 7
TILES_DEV = 28
KEEP_CAP = 11
KEEP_MOST = 19
N_ROW = 16
N_COL = 16


def keep_pattern(key, tile_rows, tile_cols, block_rows, block_cols):
    level_key = jax.random.fold_in(key, 101)
    pick_key = jax.random.fold_in(key, 202)
    levels = jax.random.randint(level_key, (tile_rows // block_rows, tile_cols // block_cols), 1, 8)
    levels = jnp.repeat(jnp.repeat(levels, block_rows, axis=0), block_cols, axis=1)
    picks = jax.random.randint(pick_key, (tile_rows, tile_cols), 0, 10)
    return (picks < levels).astype(jnp.int32)


def draw_gate_keep(key, part):
    key = jax.random.fold_in(key, 11)
    count_key = jax.random.fold_in(key, 31)
    score_key = jax.random.fold_in(key, 47)
    half_rows = N_ROW // 2
    lower = jax.random.randint(count_key, (half_rows, N_COL), 2 * KEEP_CAP - KEEP_MOST, KEEP_MOST + 1)
    lower = lower.at[0, 0].set(KEEP_MOST)
    counts = jnp.concatenate([lower, 2 * KEEP_CAP - lower], axis=0)
    scores = jax.random.randint(score_key, (N_ROW, N_COL, TILES_DEV), 0, 1048576) * TILES_DEV
    scores = scores + jnp.arange(TILES_DEV, dtype=jnp.int32)[None, None, :]
    ranks = jnp.argsort(jnp.argsort(scores, axis=-1), axis=-1)
    kept = (ranks < counts[:, :, None]).astype(jnp.int32)
    kept = kept.reshape(N_ROW, N_COL, ROW_TILES, COL_TILES).transpose(0, 2, 1, 3)
    return kept.reshape(D // TILE, FF // TILE)


def draw_down_keep(key, part):
    key = jax.random.fold_in(key, 23)
    return keep_pattern(key, FF // TILE, D // TILE, COL_TILES, ROW_TILES)


def steps_of(stream_key, extent, split, low, top_value):
    def one(axis_at, parts):
        heights = jax.random.uniform(jax.random.fold_in(jax.random.fold_in(stream_key, 6), axis_at), (parts,), jnp.float32, low / len(split), top_value / len(split))
        return jnp.repeat(jnp.exp(heights), extent[axis_at] // parts).reshape((-1,) + (1,) * (len(extent) - axis_at - 1))

    gain = one(*split[0])
    for cut in split[1:]:
        gain = gain * one(*cut)
    return gain


def scatter_about(key, shape, spread, reach, pieces=(), held_as=jnp.bfloat16):
    loudness = steps_of(key, shape, pieces, -0.22, 0.18) if pieces else 1.0
    result = jax.random.normal(key, shape, jnp.float32) * spread * loudness
    return jnp.minimum(jnp.maximum(result, -reach), reach).astype(held_as)


def setup_inputs(seed: int = 0) -> dict:
    key_list = jax.random.split(jax.random.key(seed), 10)
    return {
        "tokens": scatter_about(key_list[0], (TOKENS, D), 1.0, 6.0, ((0, 16), (1, 16))),
        "gate_codes": scatter_about(key_list[1], (D, FF), D ** -0.5, 0.046875, ((0, 16), (1, 16))),
        "gate_scale": jnp.clip(jnp.exp(math.log(5.0) - 2.3025851 * jax.random.uniform(key_list[2], (D // TILE, FF // TILE), jnp.float32) ** steps_of(key_list[2], (D // TILE, FF // TILE), ((0, 16), (1, 16)), -0.2, 0.2)), 0.5, 5.0),
        "up_codes": scatter_about(key_list[3], (D, FF), D ** -0.5, 0.046875, ((0, 16), (1, 16))),
        "up_scale": jnp.clip(jnp.exp(math.log(5.0) - 2.3025851 * jax.random.uniform(key_list[4], (D // TILE, FF // TILE), jnp.float32) ** steps_of(key_list[4], (D // TILE, FF // TILE), ((0, 16), (1, 16)), -0.2, 0.2)), 0.5, 5.0),
        "gate_keep": draw_gate_keep(jax.random.fold_in(key_list[9], 71), 0),
        "down_codes": scatter_about(key_list[6], (FF, D), FF ** -0.5, 0.03125, ((0, 16), (1, 16))),
        "down_scale": jnp.clip(jnp.exp(math.log(5.0) - 2.3025851 * jax.random.uniform(key_list[7], (FF // TILE, D // TILE), jnp.float32) ** steps_of(key_list[7], (FF // TILE, D // TILE), ((0, 16), (1, 16)), -0.2, 0.2)), 0.5, 5.0),
        "down_keep": draw_down_keep(jax.random.fold_in(key_list[9], 71), 0),
    }


def dequantize(codes, scale, keep):
    tile_rows, tile_cols = scale.shape
    rows, cols = codes.shape
    factor = scale * keep.astype(jnp.float32)
    values = codes.astype(jnp.float32).reshape(tile_rows, rows // tile_rows, tile_cols, cols // tile_cols)
    values = values * factor[:, None, :, None]
    return values.reshape(rows, cols).astype(jnp.bfloat16)


def reference(tokens, gate_codes, gate_scale, up_codes, up_scale, gate_keep, down_codes, down_scale, down_keep):
    block = D // N_ROW
    tiles = block // TILE

    def add_block(total, index):
        start = (index * block).astype(jnp.int32)
        tile_start = (index * tiles).astype(jnp.int32)
        panel = lax.dynamic_slice_in_dim(tokens, start, block, 1)
        scale_g = lax.dynamic_slice_in_dim(gate_scale, tile_start, tiles, 0)
        scale_u = lax.dynamic_slice_in_dim(up_scale, tile_start, tiles, 0)
        keep_rows = lax.dynamic_slice_in_dim(gate_keep, tile_start, tiles, 0)
        weight_g = dequantize(lax.dynamic_slice_in_dim(gate_codes, start, block, 0), scale_g, keep_rows)
        weight_u = dequantize(lax.dynamic_slice_in_dim(up_codes, start, block, 0), scale_u, keep_rows)
        term = jnp.concatenate([jnp.dot(panel, weight_g, preferred_element_type=jnp.float32),
                                jnp.dot(panel, weight_u, preferred_element_type=jnp.float32)], axis=1)
        return total + term, None

    start_total = jnp.zeros((TOKENS, 2 * FF), jnp.float32)
    sums, _ = lax.scan(add_block, start_total, jnp.arange(N_ROW, dtype=jnp.int32))
    hidden = (jax.nn.silu(sums[:, :FF]) * sums[:, FF:]).astype(jnp.bfloat16)
    weight_d = dequantize(down_codes, down_scale, down_keep)
    return jnp.dot(hidden, weight_d, preferred_element_type=jnp.float32).astype(jnp.bfloat16)
```

```python
import functools

import jax
import jax.numpy as jnp
from jax import lax
from jax.experimental import pallas as pl
from jax.experimental.pallas import tpu as pltpu
from jax.sharding import PartitionSpec as P

MESH = pl.DeviceIdType.MESH
F32 = jnp.float32
BF16 = jnp.bfloat16

X, ZL, Y, ZH, CORES = 4, 4, 4, 2, 2
GROUPS = Y
HOPS = (0, 2, 1, 3)


def kernel(
    tokens_hbm, gate_hbm, gate_scale, up_hbm, up_scale, gate_keep, down_hbm, down_scale, down_keep,
    out_ref,
    panel, w1, w2, part, relay, near, zsend, zrecv, hid, prod, sib, ysend, yrecv, own, hsend, hrecv,
    load_sem, ay_send, ay_recv, az_send, az_recv, as_send, as_recv,
    b_send, b_recv, z_send, z_recv, hz_send, hz_recv, hx_send, hx_recv,
    ds_send, ds_recv, dy_send, dy_recv, dz_send, dz_recv,
):
    rows, depth = tokens_hbm.shape
    width = gate_hbm.shape[1]
    half = width // 2
    tile = depth // gate_scale.shape[0]
    small = rows // 2

    row, col = lax.axis_index("row"), lax.axis_index("col")
    x, zl = row // ZL, row % ZL
    y, zh, core = col // (ZH * CORES), (col // CORES) % ZH, col % CORES

    def at_x(d):
        return (((x + d) % X) * ZL + zl, col)

    def at_zl(d):
        return (x * ZL + (zl + d) % ZL, col)

    def at_y(d):
        return (row, (((y + d) % Y) * ZH + zh) * CORES + core)

    across = (row, (y * ZH + (1 - zh)) * CORES + core)
    sibling = (row, (y * ZH + zh) * CORES + (1 - core))

    def remote(src, dst, send, recv, to):
        return pltpu.make_async_remote_copy(
            src_ref=src, dst_ref=dst, send_sem=send, recv_sem=recv, device_id=to, device_id_type=MESH
        )

    started = []

    def go(src, dst, send, recv, to):
        copy = remote(src, dst, send, recv, to)
        copy.start()
        started.append(copy)

    def arrive(dst, send, recv):
        remote(dst, dst, send, recv, sibling).wait_recv()

    my_block = panel.at[y, pl.ds(pl.multiple_of((zh * CORES + core) * rows, rows), rows)]
    load_tokens = pltpu.make_async_copy(tokens_hbm, my_block, load_sem.at[0])
    load_tokens.start()
    loads = []
    for u in range(2):
        for p, codes in enumerate((gate_hbm, up_hbm)):
            load = pltpu.make_async_copy(
                codes.at[:, pl.ds(u * half, half)],
                w1.at[u, :, pl.ds(p * half, half)],
                load_sem.at[1 + 2 * u + p],
            )
            load.start()
            loads.append(load)
    load_down = pltpu.make_async_copy(down_hbm, w2, load_sem.at[5])
    load_down.start()

    barrier = pltpu.get_barrier_semaphore()
    peers = [at_x(1), at_x(3), at_zl(1), at_zl(2), at_zl(3), at_y(1), at_y(2), at_y(3), across, sibling]
    for peer in peers:
        pl.semaphore_signal(barrier, inc=1, device_id=peer, device_id_type=MESH)
    pl.semaphore_wait(barrier, len(peers))

    def block(s, d):
        j = ((zh + s) % ZH) * CORES + core
        return panel.at[(y + d) % Y, pl.ds(pl.multiple_of(j * rows, rows), rows)]

    def sibling_block(s, d):
        j = ((zh + s) % ZH) * CORES + (1 - core)
        return panel.at[(y + d) % Y, pl.ds(pl.multiple_of(j * rows, rows), rows)]

    def to_sibling(s, d):
        b = block(s, d)
        go(b, b, as_send.at[s, d], as_recv.at[s, d], sibling)

    def to_columns(s):
        b = block(s, 0)
        for d in (2, 1, 3):
            go(b, b, ay_send.at[s, d], ay_recv.at[s, d], at_y(d))

    def tokens_first():
        load_tokens.wait()
        go(my_block, my_block, az_send, az_recv, across)
        to_sibling(0, 0)
        to_columns(0)

    def tokens_across():
        arrive(block(1, 0), az_send, az_recv)
        to_sibling(1, 0)
        to_columns(1)

    def tokens_of(d):
        if d:
            for s in range(2):
                back = (Y - d) % Y
                arrive(block(s, d), ay_send.at[s, back], ay_recv.at[s, back])
                to_sibling(s, d)
        for s in range(2):
            arrive(sibling_block(s, d), as_send.at[s, d], as_recv.at[s, d])

    def dequant1(u):
        for p, scale in enumerate((gate_scale, up_scale)):
            loads[2 * u + p].wait()

            @pl.loop(0, half // 128)
            def _(s):
                at = pl.ds(pl.multiple_of(p * half + s * 128, 128), 128)
                j = (u * (half // 128) + s) // (tile // 128)
                for i in range(depth // tile):
                    factor = scale[i, j] * gate_keep[i, j].astype(F32)
                    here = pl.ds(i * tile, tile)
                    w1[u, here, at] = (w1[u, here, at].astype(F32) * factor).astype(BF16)

    def dequant2():
        load_down.wait()

        @pl.loop(0, width // tile)
        def _(i):
            here = pl.ds(pl.multiple_of(i * tile, tile), tile)
            for j in range(depth // tile):
                factor = down_scale[j, i] * down_keep[j, i].astype(F32)
                at = pl.ds(j * tile, tile)
                w2[here, at] = (w2[here, at].astype(F32) * factor).astype(BF16)

    def block_rows(d):
        return pl.ds(pl.multiple_of(((x + d) % X) * rows, rows), rows)

    def product(g, u):
        yy = (y + HOPS[g]) % Y

        @pl.loop(0, width // 256)
        def _(n):
            at = pl.ds(pl.multiple_of(n * 256, 256), 256)
            part[g, u, :, at] = jnp.dot(
                panel[yy], w1[u, :, at], preferred_element_type=F32
            ).astype(BF16)

        on, plain = (1, 3) if u == 0 else (3, 1)
        go(part.at[g, u, block_rows(2)], relay.at[g, u], b_send.at[g, u, 0], b_recv.at[g, u, 0], at_x(on))
        go(part.at[g, u, block_rows(plain)], near.at[g, 1, u], b_send.at[g, u, 1], b_recv.at[g, u, 1], at_x(plain))

    def merge(g):
        for u in range(2):
            arrive(relay.at[g, u], b_send.at[g, u, 0], b_recv.at[g, u, 0])
            on = 1 if u == 0 else 3
            here = block_rows(on)
            part[g, u, here, :] = (part[g, u, here, :].astype(F32) + relay[g, u].astype(F32)).astype(BF16)
            go(part.at[g, u, here], near.at[g, 0, u], b_send.at[g, u, 2], b_recv.at[g, u, 2], at_x(on))

    mine_h, mine_u = zl // 2, zl % 2

    def sum_x(g):
        for u in range(2):
            arrive(near.at[g, 1, u], b_send.at[g, u, 1], b_recv.at[g, u, 1])
            arrive(near.at[g, 0, u], b_send.at[g, u, 2], b_recv.at[g, u, 2])
            zsend[g, u] = (
                part[g, u, block_rows(0), :].astype(F32) + near[g, 0, u].astype(F32) + near[g, 1, u].astype(F32)
            ).astype(BF16)
        for d in (2, 1, 3):
            to = (zl + d) % ZL
            go(
                zsend.at[g, to % 2, pl.ds(pl.multiple_of((to // 2) * small, small), small)],
                zrecv.at[g, d - 1], z_send.at[g, d - 1], z_recv.at[g, d - 1], at_zl(d),
            )

    def piece(z):
        return (
            pl.ds(pl.multiple_of(x * rows + (z // 2) * small, small), small),
            pl.ds(pl.multiple_of((z % 2) * half, 128), half),
        )

    def activate(g):
        for d in (1, 2, 3):
            arrive(zrecv.at[g, d - 1], z_send.at[g, d - 1], z_recv.at[g, d - 1])
        in_block = pl.ds(pl.multiple_of(mine_h * small, small), small)
        in_group = pl.ds(pl.multiple_of(x * rows + mine_h * small, small), small)

        def total(at):
            t = part[g, mine_u, in_group, at].astype(F32)
            t += near[g, 0, mine_u, in_block, at].astype(F32) + near[g, 1, mine_u, in_block, at].astype(F32)
            for d in range(3):
                t += zrecv[g, d, :, at].astype(F32)
            return t

        gate, up = total(pl.ds(0, half)), total(pl.ds(half, half))
        at_rows, at_cols = piece(zl)
        hid[g, at_rows, at_cols] = (gate / (1.0 + jnp.exp(-gate)) * up).astype(BF16)
        for d in (2, 1, 3):
            there = hid.at[g, at_rows, at_cols]
            go(there, there, hz_send.at[g, d - 1], hz_recv.at[g, d - 1], at_zl(d))

    def spread(g):
        for d in (1, 2, 3):
            at_rows, at_cols = piece((zl + ZL - d) % ZL)
            arrive(hid.at[g, at_rows, at_cols], hz_send.at[g, d - 1], hz_recv.at[g, d - 1])
        there = hid.at[g, block_rows(0)]
        go(there, there, hx_send.at[g, 0], hx_recv.at[g, 0], at_x(1))
        go(there, there, hx_send.at[g, 1], hx_recv.at[g, 1], at_x(3))

    def forward(g):
        for k, (source, to) in enumerate(((3, 1), (1, 3))):
            arrive(hid.at[g, block_rows(source)], hx_send.at[g, k], hx_recv.at[g, k])
            there = hid.at[g, block_rows(source), pl.ds(k * half, half)]
            go(there, there, hx_send.at[g, 2 + k], hx_recv.at[g, 2 + k], at_x(to))

    def down(g):
        for k in range(2):
            there = hid.at[g, block_rows(2), pl.ds(k * half, half)]
            arrive(there, hx_send.at[g, 2 + k], hx_recv.at[g, 2 + k])

        @pl.loop(0, depth // 256)
        def _(n):
            at = pl.ds(pl.multiple_of(n * 256, 256), 256)
            prod[g, :, :, at] = jnp.dot(
                hid[g], w2[:, at], preferred_element_type=F32
            ).reshape(ZH * CORES, rows, 256)

        for z in range(2):
            go(prod.at[g, z * CORES + (1 - core)], sib.at[g, z], ds_send.at[g, z], ds_recv.at[g, z], sibling)

    def to_owner(g):
        for z in range(2):
            arrive(sib.at[g, z], ds_send.at[g, z], ds_recv.at[g, z])
            s = prod[g, z * CORES + core] + sib[g, z]
            if HOPS[g]:
                ysend[g, z] = s.astype(BF16)
            else:
                own[z] = s
        if HOPS[g]:
            go(ysend.at[g], yrecv.at[g], dy_send.at[g], dy_recv.at[g], at_y(HOPS[g]))

    def finish():
        for g in range(GROUPS):
            if HOPS[g]:
                arrive(yrecv.at[g], dy_send.at[g], dy_recv.at[g])

        def total(z):
            t = own[z]
            for g in range(GROUPS):
                if HOPS[g]:
                    t += yrecv[g, z].astype(F32)
            return t

        hsend[...] = total(1 - zh).astype(BF16)
        go(hsend, hrecv, dz_send, dz_recv, across)
        kept = total(zh)
        arrive(hrecv, dz_send, dz_recv)
        out_ref[...] = (kept + hrecv[...].astype(F32)).astype(BF16)

    tokens_first()
    dequant1(0)
    tokens_across()
    dequant1(1)
    for t in range(GROUPS + 4):
        if t < GROUPS:
            tokens_of(HOPS[t])
            product(t, 0)
            product(t, 1)
        if t == 0:
            dequant2()
        if 0 <= t - 2 < GROUPS:
            activate(t - 2)
        if t < GROUPS:
            merge(t)
        if 0 <= t - 1 < GROUPS:
            sum_x(t - 1)
        if 0 <= t - 2 < GROUPS:
            spread(t - 2)
        if 0 <= t - 3 < GROUPS:
            forward(t - 3)
            down(t - 3)
        if 0 <= t - 4 < GROUPS:
            to_owner(t - 4)
    finish()
    for copy in started:
        copy.wait_send()


def per_device(
    tokens, gate_codes, gate_scale, up_codes, up_scale, gate_keep, down_codes, down_scale, down_keep
):
    rows, depth = tokens.shape
    width = gate_codes.shape[1]
    half, small, group = width // 2, rows // 2, rows * ZH * CORES
    hbm = pl.BlockSpec(memory_space=pl.ANY)
    smem = pl.BlockSpec(memory_space=pltpu.SMEM)
    dma = pltpu.SemaphoreType.DMA
    G = GROUPS
    return pl.pallas_call(
        kernel,
        out_shape=jax.ShapeDtypeStruct((rows, depth), BF16),
        in_specs=[hbm, hbm, smem, hbm, smem, smem, hbm, smem, smem],
        out_specs=pl.BlockSpec(memory_space=pltpu.VMEM),
        scratch_shapes=[
            pltpu.VMEM((Y, group, depth), BF16),
            pltpu.VMEM((2, depth, width), BF16),
            pltpu.VMEM((width, depth), BF16),
            pltpu.VMEM((G, 2, group, width), BF16),
            pltpu.VMEM((G, 2, rows, width), BF16),
            pltpu.VMEM((G, 2, 2, rows, width), BF16),
            pltpu.VMEM((G, 2, rows, width), BF16),
            pltpu.VMEM((G, ZL - 1, small, width), BF16),
            pltpu.VMEM((G, group, width), BF16),
            pltpu.VMEM((G, ZH * CORES, rows, depth), F32),
            pltpu.VMEM((G, ZH, rows, depth), F32),
            pltpu.VMEM((G, ZH, rows, depth), BF16),
            pltpu.VMEM((G, ZH, rows, depth), BF16),
            pltpu.VMEM((ZH, rows, depth), F32),
            pltpu.VMEM((rows, depth), BF16),
            pltpu.VMEM((rows, depth), BF16),
            dma((6,)),
            dma((2, Y)), dma((2, Y)),
            dma(()), dma(()),
            dma((2, Y)), dma((2, Y)),
            dma((G, 2, 3)), dma((G, 2, 3)),
            dma((G, 3)), dma((G, 3)),
            dma((G, 3)), dma((G, 3)),
            dma((G, 4)), dma((G, 4)),
            dma((G, 2)), dma((G, 2)),
            dma((G,)), dma((G,)),
            dma(()), dma(()),
        ],
        compiler_params=pltpu.CompilerParams(
            collective_id=0, has_side_effects=True, vmem_limit_bytes=56 * 1024 * 1024
        ),
    )(tokens, gate_codes, gate_scale, up_codes, up_scale, gate_keep, down_codes, down_scale.T, down_keep.T)


def solution(mesh):
    placed = (
        P("col", "row"),
        P("row", "col"),
        P("row", "col"),
        P("row", "col"),
        P("row", "col"),
        P("row", "col"),
        P("col", "row"),
        P("col", "row"),
        P("col", "row"),
    )
    return jax.shard_map(
        per_device, mesh=mesh, in_specs=placed, out_specs=P("col", "row"), check_vma=False
    )
```

```python
import jax
import jax.numpy as jnp
from jax import lax
from jax.experimental import pallas as pl
from jax.experimental.pallas import tpu as pltpu
from jax.sharding import PartitionSpec as P

MESH = pl.DeviceIdType.MESH
F32 = jnp.float32
BF16 = jnp.bfloat16
LANES = 128

X, ZL, Y, ZH, CORES = 4, 4, 4, 2, 2
UNITS = ((1, 0), (3, 0), (2, 0), (1, 1), (3, 1), (2, 1), (0, 1), (0, 0))
N = len(UNITS)
SLOT = {unit: i for i, unit in enumerate(UNITS)}


def kernel(
    tokens_hbm, gate_hbm, gate_scale, up_hbm, up_scale, gate_keep, down_hbm, down_scale, down_keep,
    out_ref,
    panel, raw, w1, w2, acc, part, relay, near, xsum, zsend, zrecv, hid, prod, sib, ysend, yrecv, own, hsend, hrecv,
    load_sem, ay_send, ay_recv, az_send, az_recv, as_send, as_recv,
    b_send, b_recv, z_send, z_recv, hz_send, hz_recv, hx_send, hx_recv,
    ds_send, ds_recv, dy_send, dy_recv, dz_send, dz_recv,
):
    rows, depth = tokens_hbm.shape
    width = gate_hbm.shape[1]
    tile = depth // gate_scale.shape[0]
    small = rows * CORES // X
    pairs = width // LANES
    share = -(-pairs // ZL)
    piece, hpiece = share * 2 * LANES, share * LANES

    row, col = lax.axis_index("row"), lax.axis_index("col")
    x, zl = row // ZL, row % ZL
    y, zh, core = col // (ZH * CORES), (col // CORES) % ZH, col % CORES

    def at_x(d):
        return (((x + d) % X) * ZL + zl, col)

    def at_zl(d):
        return (x * ZL + (zl + d) % ZL, col)

    def at_y(d):
        return (row, (((y + d) % Y) * ZH + zh) * CORES + core)

    across = (row, (y * ZH + (1 - zh)) * CORES + core)
    sibling = (row, (y * ZH + zh) * CORES + (1 - core))

    def remote(src, dst, send, recv, to):
        return pltpu.make_async_remote_copy(
            src_ref=src, dst_ref=dst, send_sem=send, recv_sem=recv, device_id=to, device_id_type=MESH
        )

    started = []

    def go(src, dst, send, recv, to):
        copy = remote(src, dst, send, recv, to)
        copy.start()
        started.append(copy)

    def arrive(dst, send, recv):
        remote(dst, dst, send, recv, sibling).wait_recv()

    def slot(d, s, c):
        return panel.at[SLOT[d, s], pl.ds(pl.multiple_of(c * rows, rows), rows)]

    mine = slot(0, 0, core)
    load_tokens = pltpu.make_async_copy(tokens_hbm, mine, load_sem.at[0])
    load_tokens.start()
    loads = []
    for p, codes in enumerate((gate_hbm, up_hbm)):
        load = pltpu.make_async_copy(codes, raw.at[p], load_sem.at[1 + p])
        load.start()
        loads.append(load)
    load_down = pltpu.make_async_copy(down_hbm, w2, load_sem.at[3])
    load_down.start()

    barrier = pltpu.get_barrier_semaphore()
    peers = [at_x(1), at_x(3), at_zl(1), at_zl(2), at_zl(3), at_y(1), at_y(2), at_y(3), across, sibling]
    for peer in peers:
        pl.semaphore_signal(barrier, inc=1, device_id=peer, device_id_type=MESH)
    pl.semaphore_wait(barrier, len(peers))

    def to_sibling(d, s):
        i = SLOT[d, s]
        go(slot(d, s, core), slot(d, s, core), as_send.at[i], as_recv.at[i], sibling)

    def to_columns(s):
        for d in (1, 3, 2):
            i = SLOT[d, s]
            go(slot(0, s, core), slot(d, s, core), ay_send.at[i], ay_recv.at[i], at_y(Y - d))

    def tokens_first():
        load_tokens.wait()
        to_columns(0)
        go(mine, slot(0, 1, core), az_send, az_recv, across)
        to_sibling(0, 0)

    def tokens_across():
        arrive(slot(0, 1, core), az_send, az_recv)
        to_columns(1)
        to_sibling(0, 1)

    def tokens_in(i):
        d, s = UNITS[i]
        if d:
            arrive(slot(d, s, core), ay_send.at[i], ay_recv.at[i])
            to_sibling(d, s)

    def tokens_all(i):
        d, s = UNITS[i]
        arrive(slot(d, s, 1 - core), as_send.at[i], as_recv.at[i])

    def dequant1():
        for load in loads:
            load.wait()

        @pl.loop(0, pairs)
        def _(t):
            j = t // (tile // LANES)
            at = pl.ds(pl.multiple_of(t * LANES, LANES), LANES)
            for p, scale in enumerate((gate_scale, up_scale)):
                to = pl.ds(pl.multiple_of(t * 2 * LANES + p * LANES, LANES), LANES)
                for i in range(depth // tile):
                    factor = scale[i, j] * gate_keep[i, j].astype(F32)
                    here = pl.ds(i * tile, tile)
                    w1[here, to] = (raw[p, here, at].astype(F32) * factor).astype(BF16)

    def dequant2():
        load_down.wait()

        @pl.loop(0, width // tile)
        def _(i):
            here = pl.ds(pl.multiple_of(i * tile, tile), tile)
            for j in range(depth // tile):
                factor = down_scale[j, i] * down_keep[j, i].astype(F32)
                at = pl.ds(j * tile, tile)
                w2[here, at] = (w2[here, at].astype(F32) * factor).astype(BF16)

    def block(d):
        return pl.ds(pl.multiple_of(((x + d) % X) * small, small), small)

    def cols(u):
        return pl.ds(u * width, width)

    def product(i):
        for u in range(2):
            t = jnp.dot(panel[i], w1[:, cols(u)], preferred_element_type=F32)
            acc[i, :, cols(u)] = t
            part[i, :, cols(u)] = t.astype(BF16)
            on, plain = (1, 3) if u == 0 else (3, 1)
            go(part.at[i, block(2), cols(u)], relay.at[i, u], b_send.at[i, u], b_recv.at[i, u], at_x(on))
            go(
                part.at[i, block(plain), cols(u)], near.at[i, 1, :, cols(u)],
                b_send.at[i, 2 + u], b_recv.at[i, 2 + u], at_x(plain),
            )

    def merge(i):
        for u in range(2):
            arrive(relay.at[i, u], b_send.at[i, u], b_recv.at[i, u])
            here = block(1 if u == 0 else 3)
            part[i, here, cols(u)] = (acc[i, here, cols(u)] + relay[i, u].astype(F32)).astype(BF16)
            go(
                part.at[i, here, cols(u)], near.at[i, 0, :, cols(u)],
                b_send.at[i, 4 + u], b_recv.at[i, 4 + u], at_x(1 if u == 0 else 3),
            )

    def sum_x(i):
        for u in range(2):
            arrive(near.at[i, 1, :, cols(u)], b_send.at[i, 2 + u], b_recv.at[i, 2 + u])
            arrive(near.at[i, 0, :, cols(u)], b_send.at[i, 4 + u], b_recv.at[i, 4 + u])
        both = pl.ds(0, 2 * width)
        t = acc[i, block(0), :] + near[i, 0].astype(F32) + near[i, 1].astype(F32)
        xsum[i, :, both] = t
        zsend[i, :, both] = t.astype(BF16)
        for d in (2, 1, 3):
            to = pl.multiple_of(((zl + d) % ZL) * piece, piece)
            go(
                zsend.at[i, :, pl.ds(to, piece)], zrecv.at[i, d - 1],
                z_send.at[i, d - 1], z_recv.at[i, d - 1], at_zl(d),
            )

    def hidden_piece(i, d):
        at = pl.multiple_of(((zl + d) % ZL) * hpiece, hpiece)
        return hid.at[i, block(0), pl.ds(at, hpiece)]

    def activate(i):
        for d in range(1, ZL):
            arrive(zrecv.at[i, d - 1], z_send.at[i, d - 1], z_recv.at[i, d - 1])
        t = xsum[i, :, pl.ds(pl.multiple_of(zl * piece, piece), piece)]
        for d in range(1, ZL):
            t += zrecv[i, d - 1].astype(F32)
        for p in range(share):
            gate = t[:, 2 * p * LANES : (2 * p + 1) * LANES]
            up = t[:, (2 * p + 1) * LANES : (2 * p + 2) * LANES]
            at = pl.ds(pl.multiple_of(zl * hpiece + p * LANES, LANES), LANES)
            hid[i, block(0), at] = (gate / (1.0 + jnp.exp(-gate)) * up).astype(BF16)
        here = hidden_piece(i, 0)
        for d in (2, 1, 3):
            go(here, here, hz_send.at[i, d - 1], hz_recv.at[i, d - 1], at_zl(d))

    def spread(i):
        for d in range(1, ZL):
            arrive(hidden_piece(i, ZL - d), hz_send.at[i, d - 1], hz_recv.at[i, d - 1])
        here = hid.at[i, block(0), pl.ds(0, width)]
        for k, d in enumerate((1, 3)):
            go(here, here, hx_send.at[i, k], hx_recv.at[i, k], at_x(d))

    def halves(k):
        return pl.ds(0, 2 * hpiece) if k == 0 else pl.ds(2 * hpiece, width - 2 * hpiece)

    def forward(i):
        for k, (source, to) in enumerate(((3, 1), (1, 3))):
            arrive(hid.at[i, block(source), pl.ds(0, width)], hx_send.at[i, k], hx_recv.at[i, k])
            here = hid.at[i, block(source), halves(k)]
            go(here, here, hx_send.at[i, 2 + k], hx_recv.at[i, 2 + k], at_x(to))

    def down(i):
        for k in range(2):
            arrive(hid.at[i, block(2), halves(k)], hx_send.at[i, 2 + k], hx_recv.at[i, 2 + k])
        t = jnp.dot(hid[i, :, pl.ds(0, width)], w2[...], preferred_element_type=F32)
        prod[i] = t.reshape(CORES, rows, depth)
        go(prod.at[i, 1 - core], sib.at[i], ds_send.at[i], ds_recv.at[i], sibling)

    def to_owner(i):
        d, s = UNITS[i]
        arrive(sib.at[i], ds_send.at[i], ds_recv.at[i])
        t = prod[i, core] + sib[i]
        if d:
            ysend[i] = t.astype(BF16)
            go(ysend.at[i], yrecv.at[i], dy_send.at[i], dy_recv.at[i], at_y(d))
        else:
            own[s] = t

    def total(s):
        t = own[s]
        for i, (d, ss) in enumerate(UNITS):
            if d and ss == s:
                arrive(yrecv.at[i], dy_send.at[i], dy_recv.at[i])
                t += yrecv[i].astype(F32)
        return t

    def cross():
        hsend[...] = total(1).astype(BF16)
        go(hsend, hrecv, dz_send, dz_recv, across)

    def finish():
        t = total(0)
        arrive(hrecv, dz_send, dz_recv)
        out_ref[...] = (t + hrecv[...].astype(F32)).astype(BF16)

    tokens_first()
    pad = pl.ds(2 * width, ZL * piece - 2 * width)
    for i in range(N):
        xsum[i, :, pad] = jnp.zeros((small, ZL * piece - 2 * width), F32)
        zsend[i, :, pad] = jnp.zeros((small, ZL * piece - 2 * width), BF16)
    dequant1()
    tokens_in(0)
    tokens_in(1)
    tokens_in(2)
    tokens_across()

    def at(i):
        return 0 <= i < N

    for t in range(N + 8):
        if at(t):
            tokens_all(t)
            product(t)
        if t == 0:
            for i in range(3, N):
                tokens_in(i)
        if t == 1:
            dequant2()
        if at(t - 1):
            merge(t - 1)
        if at(t - 2):
            sum_x(t - 2)
        if at(t - 3):
            activate(t - 3)
        if at(t - 4):
            spread(t - 4)
        if at(t - 5):
            forward(t - 5)
        if at(t - 6):
            down(t - 6)
        if at(t - 7):
            to_owner(t - 7)
            if t - 7 == SLOT[0, 1]:
                cross()
    finish()
    for copy in started:
        copy.wait_send()


def per_device(
    tokens, gate_codes, gate_scale, up_codes, up_scale, gate_keep, down_codes, down_scale, down_keep
):
    rows, depth = tokens.shape
    width = gate_codes.shape[1]
    unit, small = rows * CORES, rows * CORES // X
    share = -(-(width // LANES) // ZL)
    piece, hpiece = share * 2 * LANES, share * LANES
    hbm = pl.BlockSpec(memory_space=pl.ANY)
    smem = pl.BlockSpec(memory_space=pltpu.SMEM)
    vmem, dma = pltpu.VMEM, pltpu.SemaphoreType.DMA
    return pl.pallas_call(
        kernel,
        out_shape=jax.ShapeDtypeStruct((rows, depth), BF16),
        in_specs=[hbm, hbm, smem, hbm, smem, smem, hbm, smem, smem],
        out_specs=pl.BlockSpec(memory_space=pltpu.VMEM),
        scratch_shapes=[
            vmem((N, unit, depth), BF16),
            vmem((2, depth, width), BF16),
            vmem((depth, 2 * width), BF16),
            vmem((width, depth), BF16),
            vmem((N, unit, 2 * width), F32),
            vmem((N, unit, 2 * width), BF16),
            vmem((N, 2, small, width), BF16),
            vmem((N, 2, small, 2 * width), BF16),
            vmem((N, small, ZL * piece), F32),
            vmem((N, small, ZL * piece), BF16),
            vmem((N, ZL - 1, small, piece), BF16),
            vmem((N, unit, ZL * hpiece), BF16),
            vmem((N, CORES, rows, depth), F32),
            vmem((N, rows, depth), F32),
            vmem((N, rows, depth), BF16),
            vmem((N, rows, depth), BF16),
            vmem((ZH, rows, depth), F32),
            vmem((rows, depth), BF16),
            vmem((rows, depth), BF16),
            dma((4,)),
            dma((N,)), dma((N,)),
            dma(()), dma(()),
            dma((N,)), dma((N,)),
            dma((N, 6)), dma((N, 6)),
            dma((N, 3)), dma((N, 3)),
            dma((N, 3)), dma((N, 3)),
            dma((N, 4)), dma((N, 4)),
            dma((N,)), dma((N,)),
            dma((N,)), dma((N,)),
            dma(()), dma(()),
        ],
        compiler_params=pltpu.CompilerParams(
            collective_id=0, has_side_effects=True, vmem_limit_bytes=60 * 1024 * 1024
        ),
    )(tokens, gate_codes, gate_scale, up_codes, up_scale, gate_keep, down_codes, down_scale.T, down_keep.T)


def solution(mesh):
    placed = (
        P("col", "row"),
        P("row", "col"),
        P("row", "col"),
        P("row", "col"),
        P("row", "col"),
        P("row", "col"),
        P("col", "row"),
        P("col", "row"),
        P("col", "row"),
    )
    return jax.shard_map(
        per_device, mesh=mesh, in_specs=placed, out_specs=P("col", "row"), check_vma=False
    )
```

```python
import jax
import jax.numpy as jnp
from jax import lax
from jax.experimental import pallas as pl
from jax.experimental.pallas import tpu as pltpu
from jax.sharding import PartitionSpec as P

MESH = pl.DeviceIdType.MESH
F32 = jnp.float32
BF16 = jnp.bfloat16
LANES = 128

X, ZL, Y, ZH, CORES = 4, 4, 4, 2, 2
UNITS = ((1, 0), (3, 0), (0, 1), (1, 1), (3, 1), (2, 1), (2, 0), (0, 0))
N = len(UNITS)
SLOT = {unit: i for i, unit in enumerate(UNITS)}
WARM = 18
DIRECT = (6, 7)
ORDER = (
    "P7T0P0C0P2T1S7T3M0P3T4M2T5A7S0P4M3S2P5M4A0S3",
    "P1T6A2M5S4X0X7S5M1A3P6A4A5S1X3X4S6X5D7F3F0A1",
    "F4X2F5D3A6D4X1O3F2D0D5O4X6O5O0F1D2O2O7K0D6D1O6O1",
)


def kernel(
    tokens_hbm, gate_hbm, gate_scale, up_hbm, up_scale, gate_keep, down_hbm, down_scale, down_keep,
    out_ref,
    panel, raw, w1, w2, acc, part, relay, near, xsum, zsend, zrecv, hid, prod, sib, ysend, yrecv, own, hsend, hrecv,
    load_sem, az_send, ay_send, as_send, b_send, z_send, hz_send, hx_send, ds_send, dy_send, dz_send,
    az_recv, ay_recv, as_recv, relay_recv, near_recv, z_recv, hz_recv, hx_recv, hf_recv, ds_recv, dy_recv, dz_recv,
):
    rows, depth = tokens_hbm.shape
    width = gate_hbm.shape[1]
    tile = depth // gate_scale.shape[0]
    small = rows * CORES // X
    pairs = width // LANES
    share = -(-pairs // ZL)
    piece, hpiece = share * 2 * LANES, share * LANES

    row, col = lax.axis_index("row"), lax.axis_index("col")
    x, zl = row // ZL, row % ZL
    y, zh, core = col // (ZH * CORES), (col // CORES) % ZH, col % CORES

    def at_x(d):
        return (((x + d) % X) * ZL + zl, col)

    def at_zl(d):
        return (x * ZL + (zl + d) % ZL, col)

    def at_y(d):
        return (row, (((y + d) % Y) * ZH + zh) * CORES + core)

    across = (row, (y * ZH + (1 - zh)) * CORES + core)
    sibling = (row, (y * ZH + zh) * CORES + (1 - core))

    def remote(src, dst, send, recv, to):
        return pltpu.make_async_remote_copy(
            src_ref=src, dst_ref=dst, send_sem=send, recv_sem=recv, device_id=to, device_id_type=MESH
        )

    def go(src, dst, send, recv, to):
        remote(src, dst, send, recv, to).start()

    def arrive(like, recv):
        remote(like, like, az_send, recv, sibling).wait_recv()

    def sent(like, send):
        remote(like, like, send, az_recv, sibling).wait_send()

    def slot(d, s, c):
        return panel.at[SLOT[d, s], pl.ds(pl.multiple_of(c * rows, rows), rows)]

    mine = slot(0, 0, core)
    load_tokens = pltpu.make_async_copy(tokens_hbm, mine, load_sem.at[0])
    load_tokens.start()
    loads = []
    for p, codes in enumerate((gate_hbm, up_hbm)):
        load = pltpu.make_async_copy(codes, raw.at[p], load_sem.at[1 + p])
        load.start()
        loads.append(load)
    load_down = pltpu.make_async_copy(down_hbm, w2, load_sem.at[3])
    load_down.start()

    barrier = pltpu.get_barrier_semaphore()
    peers = [at_x(1), at_x(2), at_x(3), at_zl(1), at_zl(2), at_zl(3), at_y(1), at_y(2), at_y(3), across, sibling]
    for peer in peers:
        pl.semaphore_signal(barrier, inc=1, device_id=peer, device_id_type=MESH)
    pl.semaphore_wait(barrier, len(peers))

    def to_sibling(d, s):
        i = SLOT[d, s]
        go(slot(d, s, core), slot(d, s, core), as_send, as_recv.at[i], sibling)

    def to_columns(s):
        for d in (1, 3, 2):
            i = SLOT[d, s]
            go(slot(0, s, core), slot(d, s, core), ay_send, ay_recv.at[i], at_y(Y - d))

    def tokens_first():
        load_tokens.wait()
        to_columns(0)
        go(mine, slot(0, 1, core), az_send, az_recv, across)
        to_sibling(0, 0)

    def tokens_across():
        arrive(slot(0, 1, core), az_recv)
        to_columns(1)
        to_sibling(0, 1)

    def tokens_in(i):
        d, s = UNITS[i]
        if d:
            arrive(slot(d, s, core), ay_recv.at[i])
            to_sibling(d, s)

    def tokens_all(i):
        d, s = UNITS[i]
        arrive(slot(d, s, 1 - core), as_recv.at[i])

    def dequant1():
        for load in loads:
            load.wait()

        @pl.loop(0, pairs)
        def _(t):
            j = t // (tile // LANES)
            at = pl.ds(pl.multiple_of(t * LANES, LANES), LANES)
            for p, scale in enumerate((gate_scale, up_scale)):
                to = pl.ds(pl.multiple_of(t * 2 * LANES + p * LANES, LANES), LANES)
                for i in range(depth // tile):
                    factor = scale[i, j] * gate_keep[i, j].astype(F32)
                    here = pl.ds(i * tile, tile)
                    w1[here, to] = (raw[p, here, at].astype(F32) * factor).astype(BF16)

    def dequant2():
        load_down.wait()

        @pl.loop(0, width // tile)
        def _(i):
            here = pl.ds(pl.multiple_of(i * tile, tile), tile)
            for j in range(depth // tile):
                factor = down_scale[j, i] * down_keep[j, i].astype(F32)
                at = pl.ds(j * tile, tile)
                w2[here, at] = (w2[here, at].astype(F32) * factor).astype(BF16)

    def block(d):
        return pl.ds(pl.multiple_of(((x + d) % X) * small, small), small)

    def cols(u):
        return pl.ds(u * width, width)

    def product(i):
        tokens_all(i)
        for u in range(2):
            t = jnp.dot(panel[i], w1[:, cols(u)], preferred_element_type=F32)
            acc[i, :, cols(u)] = t
            part[i, :, cols(u)] = t.astype(BF16)
            if i in DIRECT:
                go(part.at[i, block(2), cols(u)], relay.at[i, u], b_send, near_recv.at[i], at_x(2))
                for k, d in enumerate((1, 3)):
                    go(part.at[i, block(d), cols(u)], near.at[i, k, :, cols(u)], b_send, near_recv.at[i], at_x(d))
                continue
            on, plain = (1, 3) if u == 0 else (3, 1)
            go(part.at[i, block(2), cols(u)], relay.at[i, u], b_send, relay_recv.at[i, u], at_x(on))
            go(
                part.at[i, block(plain), cols(u)], near.at[i, 1, :, cols(u)],
                b_send, near_recv.at[i], at_x(plain),
            )

    def merge(i):
        for u in range(2):
            arrive(relay.at[i, u], relay_recv.at[i, u])
            here = block(1 if u == 0 else 3)
            part[i, here, cols(u)] = (acc[i, here, cols(u)] + relay[i, u].astype(F32)).astype(BF16)
            go(
                part.at[i, here, cols(u)], near.at[i, 0, :, cols(u)],
                b_send, near_recv.at[i], at_x(1 if u == 0 else 3),
            )

    def sum_x(i):
        if i in DIRECT:
            arrive(part.at[i, pl.ds(0, 3 * small)], near_recv.at[i])
        else:
            arrive(near.at[i], near_recv.at[i])
        for u in range(2):
            at = cols(u)
            t = acc[i, block(0), at] + near[i, 0, :, at].astype(F32) + near[i, 1, :, at].astype(F32)
            if i in DIRECT:
                t += relay[i, u].astype(F32)
            xsum[i, :, at] = t
            zsend[i, :, at] = t.astype(BF16)
        for d in (2, 1, 3):
            to = pl.multiple_of(((zl + d) % ZL) * piece, piece)
            go(
                zsend.at[i, :, pl.ds(to, piece)], zrecv.at[i, d - 1],
                z_send, z_recv.at[i], at_zl(d),
            )

    def hidden_piece(i, d):
        at = pl.multiple_of(((zl + d) % ZL) * hpiece, hpiece)
        return hid.at[i, block(0), pl.ds(at, hpiece)]

    def activate(i):
        arrive(zrecv.at[i], z_recv.at[i])
        t = xsum[i, :, pl.ds(pl.multiple_of(zl * piece, piece), piece)]
        for d in range(1, ZL):
            t += zrecv[i, d - 1].astype(F32)
        for p in range(share):
            gate = t[:, 2 * p * LANES : (2 * p + 1) * LANES]
            up = t[:, (2 * p + 1) * LANES : (2 * p + 2) * LANES]
            at = pl.ds(pl.multiple_of(zl * hpiece + p * LANES, LANES), LANES)
            hid[i, block(0), at] = (gate / (1.0 + jnp.exp(-gate)) * up).astype(BF16)
        here = hidden_piece(i, 0)
        for d in (2, 1, 3):
            go(here, here, hz_send, hz_recv.at[i], at_zl(d))

    def spread(i):
        arrive(hid.at[i, block(0), pl.ds(0, (ZL - 1) * hpiece)], hz_recv.at[i])
        here = hid.at[i, block(0), pl.ds(0, width)]
        for d in (2, 1, 3) if i in DIRECT else (1, 3):
            go(here, here, hx_send, hx_recv.at[i], at_x(d))

    def halves(k):
        return pl.ds(0, 2 * hpiece) if k == 0 else pl.ds(2 * hpiece, width - 2 * hpiece)

    def forward(i):
        arrive(hid.at[i, pl.ds(0, 2 * small), pl.ds(0, width)], hx_recv.at[i])
        for k, (source, to) in enumerate(((3, 1), (1, 3))):
            here = hid.at[i, block(source), halves(k)]
            go(here, here, hx_send, hf_recv.at[i], at_x(to))

    def down(i):
        if i in DIRECT:
            arrive(hid.at[i, pl.ds(0, 3 * small), pl.ds(0, width)], hx_recv.at[i])
        else:
            arrive(hid.at[i, block(2), pl.ds(0, width)], hf_recv.at[i])
        t = jnp.dot(hid[i, :, pl.ds(0, width)], w2[...], preferred_element_type=F32)
        prod[i] = t.reshape(CORES, rows, depth)
        go(prod.at[i, 1 - core], sib.at[i], ds_send, ds_recv.at[i], sibling)

    def to_owner(i):
        d, s = UNITS[i]
        arrive(sib.at[i], ds_recv.at[i])
        t = prod[i, core] + sib[i]
        if d:
            ysend[i] = t.astype(BF16)
            go(ysend.at[i], yrecv.at[i], dy_send, dy_recv.at[i], at_y(d))
        else:
            own[s] = t

    def total(s):
        t = own[s]
        for i, (d, ss) in enumerate(UNITS):
            if d and ss == s:
                arrive(yrecv.at[i], dy_recv.at[i])
                t += yrecv[i].astype(F32)
        return t

    def cross():
        hsend[...] = total(1).astype(BF16)
        go(hsend, hrecv, dz_send, dz_recv, across)

    def finish():
        t = total(0)
        arrive(hrecv, dz_recv)
        out_ref[...] = (t + hrecv[...].astype(F32)).astype(BF16)

    tokens_first()
    pad = pl.ds(2 * width, ZL * piece - 2 * width)
    for i in range(N):
        xsum[i, :, pad] = jnp.zeros((small, ZL * piece - 2 * width), F32)
        zsend[i, :, pad] = jnp.zeros((small, ZL * piece - 2 * width), BF16)
    dequant1()
    stages = {
        "T": tokens_in, "C": lambda _: tokens_across(), "P": product, "M": merge, "S": sum_x, "A": activate,
        "X": spread, "F": forward, "D": down, "O": to_owner, "K": lambda _: cross(),
    }
    order = "".join(ORDER)
    for k in range(0, len(order), 2):
        stages[order[k]](int(order[k + 1]))
        if k == WARM:
            dequant2()
    finish()
    sent(mine, az_send)
    sent(panel.at[pl.ds(0, 3)], ay_send)
    sent(panel.at[pl.ds(0, 4)], as_send)
    sent(part.at[:, pl.ds(0, 3 * small)], b_send)
    sent(zrecv, z_send)
    sent(hid.at[:, pl.ds(0, small), pl.ds(0, 3 * hpiece)], hz_send)
    sent(hid.at[:, pl.ds(0, 3 * small), pl.ds(0, width)], hx_send)
    sent(sib, ds_send)
    sent(ysend.at[pl.ds(0, 6)], dy_send)
    sent(hsend, dz_send)


def per_device(
    tokens, gate_codes, gate_scale, up_codes, up_scale, gate_keep, down_codes, down_scale, down_keep
):
    rows, depth = tokens.shape
    width = gate_codes.shape[1]
    unit, small = rows * CORES, rows * CORES // X
    share = -(-(width // LANES) // ZL)
    piece, hpiece = share * 2 * LANES, share * LANES
    hbm = pl.BlockSpec(memory_space=pl.ANY)
    smem = pl.BlockSpec(memory_space=pltpu.SMEM)
    vmem, dma = pltpu.VMEM, pltpu.SemaphoreType.DMA
    return pl.pallas_call(
        kernel,
        out_shape=jax.ShapeDtypeStruct((rows, depth), BF16),
        in_specs=[hbm, hbm, smem, hbm, smem, smem, hbm, smem, smem],
        out_specs=pl.BlockSpec(memory_space=pltpu.VMEM),
        scratch_shapes=[
            vmem((N, unit, depth), BF16),
            vmem((2, depth, width), BF16),
            vmem((depth, 2 * width), BF16),
            vmem((width, depth), BF16),
            vmem((N, unit, 2 * width), F32),
            vmem((N, unit, 2 * width), BF16),
            vmem((N, 2, small, width), BF16),
            vmem((N, 2, small, 2 * width), BF16),
            vmem((N, small, ZL * piece), F32),
            vmem((N, small, ZL * piece), BF16),
            vmem((N, ZL - 1, small, piece), BF16),
            vmem((N, unit, ZL * hpiece), BF16),
            vmem((N, CORES, rows, depth), F32),
            vmem((N, rows, depth), F32),
            vmem((N, rows, depth), BF16),
            vmem((N, rows, depth), BF16),
            vmem((ZH, rows, depth), F32),
            vmem((rows, depth), BF16),
            vmem((rows, depth), BF16),
            dma((4,)),
            *[dma(())] * 10,
            dma(()), dma((N,)), dma((N,)),
            dma((N, 2)), dma((N,)),
            dma((N,)), dma((N,)),
            dma((N,)), dma((N,)),
            dma((N,)), dma((N,)), dma(()),
        ],
        compiler_params=pltpu.CompilerParams(
            collective_id=0, has_side_effects=True, vmem_limit_bytes=60 * 1024 * 1024
        ),
    )(tokens, gate_codes, gate_scale, up_codes, up_scale, gate_keep, down_codes, down_scale.T, down_keep.T)


def solution(mesh):
    placed = (
        P("col", "row"),
        P("row", "col"),
        P("row", "col"),
        P("row", "col"),
        P("row", "col"),
        P("row", "col"),
        P("col", "row"),
        P("col", "row"),
        P("col", "row"),
    )
    return jax.shard_map(
        per_device, mesh=mesh, in_specs=placed, out_specs=P("col", "row"), check_vma=False
    )
```

```python
import jax
import jax.numpy as jnp
from jax import lax
from jax.experimental import pallas as pl
from jax.experimental.pallas import tpu as pltpu
from jax.sharding import PartitionSpec as P

MESH = pl.DeviceIdType.MESH
F32 = jnp.float32
BF16 = jnp.bfloat16
LANES = 128

X, ZL, Y, ZH, CORES = 4, 4, 4, 2, 2
UNITS = ((1, 0), (3, 0), (0, 1), (1, 1), (3, 1), (2, 1), (2, 0), (0, 0))
N = len(UNITS)
SLOT = {unit: i for i, unit in enumerate(UNITS)}
WARM = 18
DIRECT = (6, 7)
ORDER = (
    "P7T0P0C0P2T3M0P3T5T1M2T4S7P5S0M3P4S2A7T6M5P1S3",
    "M4A0X7S5M1A2A3P6S4A5S1X2D7X0A4X3X5S6F2A1X4F3F5",
    "A6D2F4X1F0D3D5X6O3D4O5F1O7O4O2D0D6D1K0O6O0O1",
)


def kernel(
    tokens_hbm, gate_hbm, gate_scale, up_hbm, up_scale, gate_keep, down_hbm, down_scale, down_keep,
    out_ref,
    panel, raw, w1, w2, acc, part, relay, near, xsum, zsend, zrecv, hid, prod, sib, ysend, yrecv, own, hsend, hrecv,
    load_sem, az_send, ay_send, as_send, b_send, z_send, hz_send, hx_send, ds_send, dy_send, dz_send,
    az_recv, ay_recv, as_recv, relay_recv, near_recv, z_recv, hz_recv, hx_recv, hf_recv, ds_recv, dy_recv, dz_recv,
):
    rows, depth = tokens_hbm.shape
    width = gate_hbm.shape[1]
    tile = depth // gate_scale.shape[0]
    small = rows * CORES // X
    pairs = width // LANES
    base = pairs // ZL
    wide, narrow = (base + 1) * LANES, base * LANES

    row, col = lax.axis_index("row"), lax.axis_index("col")
    x, zl = row // ZL, row % ZL
    y, zh, core = col // (ZH * CORES), (col // CORES) % ZH, col % CORES

    even = zl % 2 == 0

    def by_parity(f):
        pl.when(even)(lambda: f(wide, narrow))
        pl.when(jnp.logical_not(even))(lambda: f(narrow, wide))

    def first(z, k):
        return pl.multiple_of((base * z + (z + 1) // 2) * (k * LANES), k * LANES)

    def at_x(d):
        return (((x + d) % X) * ZL + zl, col)

    def at_zl(d):
        return (x * ZL + (zl + d) % ZL, col)

    def at_y(d):
        return (row, (((y + d) % Y) * ZH + zh) * CORES + core)

    across = (row, (y * ZH + (1 - zh)) * CORES + core)
    sibling = (row, (y * ZH + zh) * CORES + (1 - core))

    def remote(src, dst, send, recv, to):
        return pltpu.make_async_remote_copy(
            src_ref=src, dst_ref=dst, send_sem=send, recv_sem=recv, device_id=to, device_id_type=MESH
        )

    def go(src, dst, send, recv, to):
        remote(src, dst, send, recv, to).start()

    def arrive(like, recv):
        remote(like, like, az_send, recv, sibling).wait_recv()

    def sent(like, send):
        remote(like, like, send, az_recv, sibling).wait_send()

    def slot(d, s, c):
        return panel.at[SLOT[d, s], pl.ds(pl.multiple_of(c * rows, rows), rows)]

    mine = slot(0, 0, core)
    load_tokens = pltpu.make_async_copy(tokens_hbm, mine, load_sem.at[0])
    load_tokens.start()
    loads = []
    for i in range(depth // tile):
        here = pl.ds(i * tile, tile)
        for p, codes in enumerate((gate_hbm, up_hbm)):
            load = pltpu.make_async_copy(codes.at[here], raw.at[p, here], load_sem.at[2 + 2 * i + p])
            load.start()
            loads.append(load)
    load_down = pltpu.make_async_copy(down_hbm, w2, load_sem.at[1])
    load_down.start()

    barrier = pltpu.get_barrier_semaphore()
    peers = [at_x(1), at_x(2), at_x(3), at_zl(1), at_zl(2), at_zl(3), at_y(1), at_y(2), at_y(3), across, sibling]
    for peer in peers:
        pl.semaphore_signal(barrier, inc=1, device_id=peer, device_id_type=MESH)

    def to_sibling(d, s):
        i = SLOT[d, s]
        go(slot(d, s, core), slot(d, s, core), as_send, as_recv.at[i], sibling)

    def to_columns(s):
        for d in (1, 3, 2):
            i = SLOT[d, s]
            go(slot(0, s, core), slot(d, s, core), ay_send, ay_recv.at[i], at_y(Y - d))

    def tokens_first():
        load_tokens.wait()
        to_columns(0)
        go(mine, slot(0, 1, core), az_send, az_recv, across)
        to_sibling(0, 0)

    def tokens_across():
        arrive(slot(0, 1, core), az_recv)
        to_columns(1)
        to_sibling(0, 1)

    def tokens_in(i):
        d, s = UNITS[i]
        if d:
            arrive(slot(d, s, core), ay_recv.at[i])
            to_sibling(d, s)

    def tokens_all(i):
        d, s = UNITS[i]
        arrive(slot(d, s, 1 - core), as_recv.at[i])

    def dequant1(tiles):
        for i in tiles:
            here = pl.ds(i * tile, tile)
            for p in range(2):
                loads[2 * i + p].wait()

            @pl.loop(0, pairs)
            def _(t):
                j = t // (tile // LANES)
                at = pl.ds(pl.multiple_of(t * LANES, LANES), LANES)
                for p, scale in enumerate((gate_scale, up_scale)):
                    to = pl.ds(pl.multiple_of(t * 2 * LANES + p * LANES, LANES), LANES)
                    factor = scale[i, j] * gate_keep[i, j].astype(F32)
                    w1[here, to] = (raw[p, here, at].astype(F32) * factor).astype(BF16)

    def dequant2():
        load_down.wait()

        @pl.loop(0, width // tile)
        def _(i):
            here = pl.ds(pl.multiple_of(i * tile, tile), tile)
            for j in range(depth // tile):
                factor = down_scale[j, i] * down_keep[j, i].astype(F32)
                at = pl.ds(j * tile, tile)
                w2[here, at] = (w2[here, at].astype(F32) * factor).astype(BF16)

    def block(d):
        return pl.ds(pl.multiple_of(((x + d) % X) * small, small), small)

    def cols(u):
        return pl.ds(u * width, width)

    def product(i):
        tokens_all(i)
        for u in range(2):
            t = jnp.dot(panel[i], w1[:, cols(u)], preferred_element_type=F32)
            acc[i, :, cols(u)] = t
            part[i, :, cols(u)] = t.astype(BF16)
            if i in DIRECT:
                go(part.at[i, block(2), cols(u)], relay.at[i, u], b_send, near_recv.at[i], at_x(2))
                for k, d in enumerate((1, 3)):
                    go(part.at[i, block(d), cols(u)], near.at[i, k, :, cols(u)], b_send, near_recv.at[i], at_x(d))
                continue
            on, plain = (1, 3) if u == 0 else (3, 1)
            go(part.at[i, block(2), cols(u)], relay.at[i, u], b_send, relay_recv.at[i, u], at_x(on))
            go(
                part.at[i, block(plain), cols(u)], near.at[i, 1, :, cols(u)],
                b_send, near_recv.at[i], at_x(plain),
            )

    def merge(i):
        for u in range(2):
            arrive(relay.at[i, u], relay_recv.at[i, u])
            here = block(1 if u == 0 else 3)
            part[i, here, cols(u)] = (acc[i, here, cols(u)] + relay[i, u].astype(F32)).astype(BF16)
            go(
                part.at[i, here, cols(u)], near.at[i, 0, :, cols(u)],
                b_send, near_recv.at[i], at_x(1 if u == 0 else 3),
            )

    def sum_x(i):
        if i in DIRECT:
            arrive(part.at[i, pl.ds(0, 3 * small)], near_recv.at[i])
        else:
            arrive(near.at[i], near_recv.at[i])
        for u in range(2):
            at = cols(u)
            t = acc[i, block(0), at] + near[i, 0, :, at].astype(F32) + near[i, 1, :, at].astype(F32)
            if i in DIRECT:
                t += relay[i, u].astype(F32)
            xsum[i, :, at] = t
            zsend[i, :, at] = t.astype(BF16)

        def send(same, other):
            for d in (2, 1, 3):
                lanes = 2 * (other if d % 2 else same)
                at = first((zl + d) % ZL, 2)
                go(
                    zsend.at[i, :, pl.ds(at, lanes)], zrecv.at[i, d - 1, :, pl.ds(0, lanes)],
                    z_send, z_recv.at[i], at_zl(d),
                )

        by_parity(send)

    def activate(i):
        by_parity(lambda same, _: arrive(zrecv.at[i, :, :, pl.ds(0, 2 * same)], z_recv.at[i]))

        def pair(p):
            def total(k):
                t = xsum[i, :, pl.ds(pl.multiple_of(first(zl, 2) + k * LANES, LANES), LANES)]
                for d in range(1, ZL):
                    t += zrecv[i, d - 1, :, pl.ds(k * LANES, LANES)].astype(F32)
                return t

            gate, up = total(2 * p), total(2 * p + 1)
            at = pl.ds(pl.multiple_of(first(zl, 1) + p * LANES, LANES), LANES)
            hid[i, block(0), at] = (gate / (1.0 + jnp.exp(-gate)) * up).astype(BF16)

        for p in range(base):
            pair(p)
        pl.when(even)(lambda: pair(base))

        def send(same, _):
            here = hid.at[i, block(0), pl.ds(first(zl, 1), same)]
            for d in (2, 1, 3):
                go(here, here, hz_send, hz_recv.at[i], at_zl(d))

        by_parity(send)

    def spread(i):
        by_parity(lambda same, other: arrive(hid.at[i, block(0), pl.ds(0, same + 2 * other)], hz_recv.at[i]))
        here = hid.at[i, block(0), pl.ds(0, width)]
        for d in (2, 1, 3) if i in DIRECT else (1, 3):
            go(here, here, hx_send, hx_recv.at[i], at_x(d))

    def halves(k):
        return pl.ds(k * (width // 2), width // 2)

    def forward(i):
        arrive(hid.at[i, pl.ds(0, 2 * small), pl.ds(0, width)], hx_recv.at[i])
        for k, (source, to) in enumerate(((3, 1), (1, 3))):
            here = hid.at[i, block(source), halves(k)]
            go(here, here, hx_send, hf_recv.at[i], at_x(to))

    def down(i):
        if i in DIRECT:
            arrive(hid.at[i, pl.ds(0, 3 * small), pl.ds(0, width)], hx_recv.at[i])
        else:
            arrive(hid.at[i, block(2), pl.ds(0, width)], hf_recv.at[i])
        t = jnp.dot(hid[i, :, pl.ds(0, width)], w2[...], preferred_element_type=F32)
        prod[i] = t.reshape(CORES, rows, depth)
        go(prod.at[i, 1 - core], sib.at[i], ds_send, ds_recv.at[i], sibling)

    def to_owner(i):
        d, s = UNITS[i]
        arrive(sib.at[i], ds_recv.at[i])
        t = prod[i, core] + sib[i]
        if d:
            ysend[i] = t.astype(BF16)
            go(ysend.at[i], yrecv.at[i], dy_send, dy_recv.at[i], at_y(d))
        else:
            own[s] = t

    def total(s):
        t = own[s]
        for i, (d, ss) in enumerate(UNITS):
            if d and ss == s:
                arrive(yrecv.at[i], dy_recv.at[i])
                t += yrecv[i].astype(F32)
        return t

    def cross():
        hsend[...] = total(1).astype(BF16)
        go(hsend, hrecv, dz_send, dz_recv, across)

    def finish():
        t = total(0)
        arrive(hrecv, dz_recv)
        out_ref[...] = (t + hrecv[...].astype(F32)).astype(BF16)

    dequant1(range(2))
    pl.semaphore_wait(barrier, len(peers))
    tokens_first()
    dequant1(range(2, depth // tile))
    stages = {
        "T": tokens_in, "C": lambda _: tokens_across(), "P": product, "M": merge, "S": sum_x, "A": activate,
        "X": spread, "F": forward, "D": down, "O": to_owner, "K": lambda _: cross(),
    }
    order = "".join(ORDER)
    for k in range(0, len(order), 2):
        stages[order[k]](int(order[k + 1]))
        if k == WARM:
            dequant2()
    finish()
    sent(mine, az_send)
    sent(panel.at[pl.ds(0, 3)], ay_send)
    sent(panel.at[pl.ds(0, 4)], as_send)
    sent(part.at[:, pl.ds(0, 3 * small)], b_send)
    by_parity(lambda same, other: sent(zsend.at[:, :, pl.ds(0, 2 * same + 4 * other)], z_send))
    by_parity(lambda same, _: sent(hid.at[:, pl.ds(0, small), pl.ds(0, 3 * same)], hz_send))
    sent(hid.at[:, pl.ds(0, 3 * small), pl.ds(0, width)], hx_send)
    sent(sib, ds_send)
    sent(ysend.at[pl.ds(0, 6)], dy_send)
    sent(hsend, dz_send)


def per_device(
    tokens, gate_codes, gate_scale, up_codes, up_scale, gate_keep, down_codes, down_scale, down_keep
):
    rows, depth = tokens.shape
    width = gate_codes.shape[1]
    unit, small = rows * CORES, rows * CORES // X
    piece = (width // LANES // ZL + 1) * 2 * LANES
    hbm = pl.BlockSpec(memory_space=pl.ANY)
    smem = pl.BlockSpec(memory_space=pltpu.SMEM)
    vmem, dma = pltpu.VMEM, pltpu.SemaphoreType.DMA
    return pl.pallas_call(
        kernel,
        out_shape=jax.ShapeDtypeStruct((rows, depth), BF16),
        in_specs=[hbm, hbm, smem, hbm, smem, smem, hbm, smem, smem],
        out_specs=pl.BlockSpec(memory_space=pltpu.VMEM),
        scratch_shapes=[
            vmem((N, unit, depth), BF16),
            vmem((2, depth, width), BF16),
            vmem((depth, 2 * width), BF16),
            vmem((width, depth), BF16),
            vmem((N, unit, 2 * width), F32),
            vmem((N, unit, 2 * width), BF16),
            vmem((N, 2, small, width), BF16),
            vmem((N, 2, small, 2 * width), BF16),
            vmem((N, small, 2 * width), F32),
            vmem((N, small, 2 * width), BF16),
            vmem((N, ZL - 1, small, piece), BF16),
            vmem((N, unit, width), BF16),
            vmem((N, CORES, rows, depth), F32),
            vmem((N, rows, depth), F32),
            vmem((N, rows, depth), BF16),
            vmem((N, rows, depth), BF16),
            vmem((ZH, rows, depth), F32),
            vmem((rows, depth), BF16),
            vmem((rows, depth), BF16),
            dma((2 + 2 * gate_scale.shape[0],)),
            *[dma(())] * 10,
            dma(()), dma((N,)), dma((N,)),
            dma((N, 2)), dma((N,)),
            dma((N,)), dma((N,)),
            dma((N,)), dma((N,)),
            dma((N,)), dma((N,)), dma(()),
        ],
        compiler_params=pltpu.CompilerParams(
            collective_id=0, has_side_effects=True, vmem_limit_bytes=60 * 1024 * 1024
        ),
    )(tokens, gate_codes, gate_scale, up_codes, up_scale, gate_keep, down_codes, down_scale.T, down_keep.T)


def solution(mesh):
    placed = (
        P("col", "row"),
        P("row", "col"),
        P("row", "col"),
        P("row", "col"),
        P("row", "col"),
        P("row", "col"),
        P("col", "row"),
        P("col", "row"),
        P("col", "row"),
    )
    return jax.shard_map(
        per_device, mesh=mesh, in_specs=placed, out_specs=P("col", "row"), check_vma=False
    )
```

```python
import jax
import jax.numpy as jnp
from jax import lax
from jax.experimental import pallas as pl
from jax.experimental.pallas import tpu as pltpu
from jax.sharding import PartitionSpec as P

MESH = pl.DeviceIdType.MESH
F32 = jnp.float32
BF16 = jnp.bfloat16
LANES = 128

X, ZL, Y, ZH, CORES = 4, 4, 4, 2, 2
UNITS = ((1, 0), (3, 0), (0, 1), (1, 1), (3, 1), (2, 1), (2, 0), (0, 0))
N = len(UNITS)
SLOT = {unit: i for i, unit in enumerate(UNITS)}
WARM = 34
DIRECT = (6, 7)
LATE = (1,)
ORDER = (
    "P7T0P0C0P2T4T1S7M0T3P4M2P3T5S0M4S2P5M3A0T6S4P1",
    "M5A2X0S3A4M1P6S5X2A3X4S1A5X3S6F2A1X5F4F3F0A7A6",
    "X1D2F5D4D3O2O4X6D5O3O5X7D0D1D6K0O1O0O6D7O7",
)


def kernel(
    tokens_hbm, gate_hbm, gate_scale, up_hbm, up_scale, gate_keep, down_hbm, down_scale, down_keep,
    out_ref,
    panel, raw, w1, w2, acc, part, relay, near, xsum, zsend, zrecv, hid, prod, sib, ysend, yrecv, own, hsend, hrecv,
    load_sem, az_send, ay_send, as_send, b_send, z_send, hz_send, hx_send, hl_send, ds_send, dy_send, dz_send,
    az_recv, ay_recv, as_recv, relay_recv, near_recv, z_recv, hz_recv, hx_recv, hf_recv, ds_recv, dy_recv, dz_recv,
):
    rows, depth = tokens_hbm.shape
    width = gate_hbm.shape[1]
    tile = depth // gate_scale.shape[0]
    small = rows * CORES // X
    pairs = width // LANES
    base = pairs // ZL
    wide, narrow = (base + 1) * LANES, base * LANES

    row, col = lax.axis_index("row"), lax.axis_index("col")
    x, zl = row // ZL, row % ZL
    y, zh, core = col // (ZH * CORES), (col // CORES) % ZH, col % CORES

    even = zl % 2 == 0

    def by_parity(f):
        pl.when(even)(lambda: f(wide, narrow))
        pl.when(jnp.logical_not(even))(lambda: f(narrow, wide))

    def first(z, k):
        return pl.multiple_of((base * z + (z + 1) // 2) * (k * LANES), k * LANES)

    def at_x(d):
        return (((x + d) % X) * ZL + zl, col)

    def at_zl(d):
        return (x * ZL + (zl + d) % ZL, col)

    def at_y(d):
        return (row, (((y + d) % Y) * ZH + zh) * CORES + core)

    across = (row, (y * ZH + (1 - zh)) * CORES + core)
    sibling = (row, (y * ZH + zh) * CORES + (1 - core))

    def remote(src, dst, send, recv, to):
        return pltpu.make_async_remote_copy(
            src_ref=src, dst_ref=dst, send_sem=send, recv_sem=recv, device_id=to, device_id_type=MESH
        )

    def go(src, dst, send, recv, to):
        remote(src, dst, send, recv, to).start()

    def arrive(like, recv):
        remote(like, like, az_send, recv, sibling).wait_recv()

    def sent(like, send):
        remote(like, like, send, az_recv, sibling).wait_send()

    def slot(d, s, c):
        return panel.at[SLOT[d, s], pl.ds(pl.multiple_of(c * rows, rows), rows)]

    mine = slot(0, 0, core)
    load_tokens = pltpu.make_async_copy(tokens_hbm, mine, load_sem.at[0])
    load_tokens.start()
    loads = []
    for i in range(depth // tile):
        here = pl.ds(i * tile, tile)
        for p, codes in enumerate((gate_hbm, up_hbm)):
            load = pltpu.make_async_copy(codes.at[here], raw.at[p, here], load_sem.at[2 + 2 * i + p])
            load.start()
            loads.append(load)
    load_down = pltpu.make_async_copy(down_hbm, w2, load_sem.at[1])
    load_down.start()

    barrier = pltpu.get_barrier_semaphore()
    peers = [at_x(1), at_x(2), at_x(3), at_zl(1), at_zl(2), at_zl(3), at_y(1), at_y(2), at_y(3), across, sibling]
    for peer in peers:
        pl.semaphore_signal(barrier, inc=1, device_id=peer, device_id_type=MESH)

    def to_sibling(d, s):
        i = SLOT[d, s]
        go(slot(d, s, core), slot(d, s, core), as_send, as_recv.at[i], sibling)

    def to_columns(s):
        for d in (1, 3, 2):
            i = SLOT[d, s]
            go(slot(0, s, core), slot(d, s, core), ay_send, ay_recv.at[i], at_y(Y - d))

    def tokens_first():
        load_tokens.wait()
        to_columns(0)
        go(mine, slot(0, 1, core), az_send, az_recv, across)
        to_sibling(0, 0)

    def tokens_across():
        arrive(slot(0, 1, core), az_recv)
        to_columns(1)
        to_sibling(0, 1)

    def tokens_in(i):
        d, s = UNITS[i]
        if d:
            arrive(slot(d, s, core), ay_recv.at[i])
            to_sibling(d, s)

    def tokens_all(i):
        d, s = UNITS[i]
        arrive(slot(d, s, 1 - core), as_recv.at[i])

    def dequant1(tiles):
        for i in tiles:
            here = pl.ds(i * tile, tile)
            for p in range(2):
                loads[2 * i + p].wait()

            @pl.loop(0, pairs)
            def _(t):
                j = t // (tile // LANES)
                at = pl.ds(pl.multiple_of(t * LANES, LANES), LANES)
                for p, scale in enumerate((gate_scale, up_scale)):
                    to = pl.ds(pl.multiple_of(t * 2 * LANES + p * LANES, LANES), LANES)
                    factor = scale[i, j] * gate_keep[i, j].astype(F32)
                    w1[here, to] = (raw[p, here, at].astype(F32) * factor).astype(BF16)

    def dequant2():
        load_down.wait()

        @pl.loop(0, width // tile)
        def _(i):
            here = pl.ds(pl.multiple_of(i * tile, tile), tile)
            for j in range(depth // tile):
                factor = down_scale[j, i] * down_keep[j, i].astype(F32)
                at = pl.ds(j * tile, tile)
                w2[here, at] = (w2[here, at].astype(F32) * factor).astype(BF16)

    def block(d):
        return pl.ds(pl.multiple_of(((x + d) % X) * small, small), small)

    def cols(u):
        return pl.ds(u * width, width)

    def product(i):
        tokens_all(i)
        for u in range(2):
            t = jnp.dot(panel[i], w1[:, cols(u)], preferred_element_type=F32)
            acc[i, :, cols(u)] = t
            part[i, :, cols(u)] = t.astype(BF16)
            if i in DIRECT:
                go(part.at[i, block(2), cols(u)], relay.at[i, u], b_send, near_recv.at[i], at_x(2))
                for k, d in enumerate((1, 3)):
                    go(part.at[i, block(d), cols(u)], near.at[i, k, :, cols(u)], b_send, near_recv.at[i], at_x(d))
                continue
            on, plain = (1, 3) if u == 0 else (3, 1)
            go(part.at[i, block(2), cols(u)], relay.at[i, u], b_send, relay_recv.at[i, u], at_x(on))
            go(
                part.at[i, block(plain), cols(u)], near.at[i, 1, :, cols(u)],
                b_send, near_recv.at[i], at_x(plain),
            )

    def merge(i):
        for u in range(2):
            arrive(relay.at[i, u], relay_recv.at[i, u])
            here = block(1 if u == 0 else 3)
            part[i, here, cols(u)] = (acc[i, here, cols(u)] + relay[i, u].astype(F32)).astype(BF16)
            go(
                part.at[i, here, cols(u)], near.at[i, 0, :, cols(u)],
                b_send, near_recv.at[i], at_x(1 if u == 0 else 3),
            )

    def sum_x(i):
        if i in DIRECT:
            arrive(part.at[i, pl.ds(0, 3 * small)], near_recv.at[i])
        else:
            arrive(near.at[i], near_recv.at[i])
        for u in range(2):
            at = cols(u)
            t = acc[i, block(0), at] + near[i, 0, :, at].astype(F32) + near[i, 1, :, at].astype(F32)
            if i in DIRECT:
                t += relay[i, u].astype(F32)
            xsum[i, :, at] = t
            zsend[i, :, at] = t.astype(BF16)

        def send(same, other):
            for d in (2, 1, 3):
                lanes = 2 * (other if d % 2 else same)
                at = first((zl + d) % ZL, 2)
                go(
                    zsend.at[i, :, pl.ds(at, lanes)], zrecv.at[i, d - 1, :, pl.ds(0, lanes)],
                    z_send, z_recv.at[i], at_zl(d),
                )

        by_parity(send)

    def activate(i):
        by_parity(lambda same, _: arrive(zrecv.at[i, :, :, pl.ds(0, 2 * same)], z_recv.at[i]))

        def pair(p):
            def total(k):
                t = xsum[i, :, pl.ds(pl.multiple_of(first(zl, 2) + k * LANES, LANES), LANES)]
                for d in range(1, ZL):
                    t += zrecv[i, d - 1, :, pl.ds(k * LANES, LANES)].astype(F32)
                return t

            gate, up = total(2 * p), total(2 * p + 1)
            at = pl.ds(pl.multiple_of(first(zl, 1) + p * LANES, LANES), LANES)
            hid[i, block(0), at] = (gate / (1.0 + jnp.exp(-gate)) * up).astype(BF16)

        for p in range(base):
            pair(p)
        pl.when(even)(lambda: pair(base))

        def send(same, _):
            here = hid.at[i, block(0), pl.ds(first(zl, 1), same)]
            for d in (2, 1, 3):
                go(here, here, hz_send, hz_recv.at[i], at_x(d) if i in LATE else at_zl(d))

        by_parity(send)

    def spread_late(i):
        by_parity(lambda same, _: arrive(hid.at[i, block(0), pl.ds(0, 3 * same)], hz_recv.at[i]))

        def send(same, _):
            here = hid.at[i, :, pl.ds(first(zl, 1), same)]
            for d in (2, 1, 3):
                go(here, here, hl_send, hx_recv.at[i], at_zl(d))

        by_parity(send)

    def spread(i):
        if i in LATE:
            return spread_late(i)
        by_parity(lambda same, other: arrive(hid.at[i, block(0), pl.ds(0, same + 2 * other)], hz_recv.at[i]))
        here = hid.at[i, block(0), pl.ds(0, width)]
        for d in (2, 1, 3) if i in DIRECT else (1, 3):
            go(here, here, hx_send, hx_recv.at[i], at_x(d))

    def halves(k):
        return pl.ds(k * (width // 2), width // 2)

    def forward(i):
        arrive(hid.at[i, pl.ds(0, 2 * small), pl.ds(0, width)], hx_recv.at[i])
        for k, (source, to) in enumerate(((3, 1), (1, 3))):
            here = hid.at[i, block(source), halves(k)]
            go(here, here, hx_send, hf_recv.at[i], at_x(to))

    def down(i):
        if i in LATE:
            by_parity(lambda same, other: arrive(hid.at[i, :, pl.ds(0, same + 2 * other)], hx_recv.at[i]))
        elif i in DIRECT:
            arrive(hid.at[i, pl.ds(0, 3 * small), pl.ds(0, width)], hx_recv.at[i])
        else:
            arrive(hid.at[i, block(2), pl.ds(0, width)], hf_recv.at[i])
        t = jnp.dot(hid[i, :, pl.ds(0, width)], w2[...], preferred_element_type=F32)
        prod[i] = t.reshape(CORES, rows, depth)
        go(prod.at[i, 1 - core], sib.at[i], ds_send, ds_recv.at[i], sibling)

    def to_owner(i):
        d, s = UNITS[i]
        arrive(sib.at[i], ds_recv.at[i])
        t = prod[i, core] + sib[i]
        if d:
            ysend[i] = t.astype(BF16)
            go(ysend.at[i], yrecv.at[i], dy_send, dy_recv.at[i], at_y(d))
        else:
            own[s] = t

    def total(s):
        t = own[s]
        for i, (d, ss) in enumerate(UNITS):
            if d and ss == s:
                arrive(yrecv.at[i], dy_recv.at[i])
                t += yrecv[i].astype(F32)
        return t

    def cross():
        hsend[...] = total(1).astype(BF16)
        go(hsend, hrecv, dz_send, dz_recv, across)

    def finish():
        t = total(0)
        arrive(hrecv, dz_recv)
        out_ref[...] = (t + hrecv[...].astype(F32)).astype(BF16)

    dequant1(range(2))
    pl.semaphore_wait(barrier, len(peers))
    tokens_first()
    dequant1(range(2, depth // tile))
    stages = {
        "T": tokens_in, "C": lambda _: tokens_across(), "P": product, "M": merge, "S": sum_x, "A": activate,
        "X": spread, "F": forward, "D": down, "O": to_owner, "K": lambda _: cross(),
    }
    order = "".join(ORDER)
    for k in range(0, len(order), 2):
        stages[order[k]](int(order[k + 1]))
        if k == WARM:
            dequant2()
    finish()
    sent(mine, az_send)
    sent(panel.at[pl.ds(0, 3)], ay_send)
    sent(panel.at[pl.ds(0, 4)], as_send)
    sent(part.at[:, pl.ds(0, 3 * small)], b_send)
    by_parity(lambda same, other: sent(zsend.at[:, :, pl.ds(0, 2 * same + 4 * other)], z_send))
    by_parity(lambda same, _: sent(hid.at[:, pl.ds(0, small), pl.ds(0, 3 * same)], hz_send))
    sent(hid.at[pl.ds(0, N - len(LATE)), pl.ds(0, 3 * small), pl.ds(0, width)], hx_send)
    by_parity(lambda same, _: sent(hid.at[pl.ds(0, len(LATE)), :, pl.ds(0, 3 * same)], hl_send))
    sent(sib, ds_send)
    sent(ysend.at[pl.ds(0, 6)], dy_send)
    sent(hsend, dz_send)


def per_device(
    tokens, gate_codes, gate_scale, up_codes, up_scale, gate_keep, down_codes, down_scale, down_keep
):
    rows, depth = tokens.shape
    width = gate_codes.shape[1]
    unit, small = rows * CORES, rows * CORES // X
    piece = (width // LANES // ZL + 1) * 2 * LANES
    hbm = pl.BlockSpec(memory_space=pl.ANY)
    smem = pl.BlockSpec(memory_space=pltpu.SMEM)
    vmem, dma = pltpu.VMEM, pltpu.SemaphoreType.DMA
    return pl.pallas_call(
        kernel,
        out_shape=jax.ShapeDtypeStruct((rows, depth), BF16),
        in_specs=[hbm, hbm, smem, hbm, smem, smem, hbm, smem, smem],
        out_specs=pl.BlockSpec(memory_space=pltpu.VMEM),
        scratch_shapes=[
            vmem((N, unit, depth), BF16),
            vmem((2, depth, width), BF16),
            vmem((depth, 2 * width), BF16),
            vmem((width, depth), BF16),
            vmem((N, unit, 2 * width), F32),
            vmem((N, unit, 2 * width), BF16),
            vmem((N, 2, small, width), BF16),
            vmem((N, 2, small, 2 * width), BF16),
            vmem((N, small, 2 * width), F32),
            vmem((N, small, 2 * width), BF16),
            vmem((N, ZL - 1, small, piece), BF16),
            vmem((N, unit, width), BF16),
            vmem((N, CORES, rows, depth), F32),
            vmem((N, rows, depth), F32),
            vmem((N, rows, depth), BF16),
            vmem((N, rows, depth), BF16),
            vmem((ZH, rows, depth), F32),
            vmem((rows, depth), BF16),
            vmem((rows, depth), BF16),
            dma((2 + 2 * gate_scale.shape[0],)),
            *[dma(())] * 11,
            dma(()), dma((N,)), dma((N,)),
            dma((N, 2)), dma((N,)),
            dma((N,)), dma((N,)),
            dma((N,)), dma((N,)),
            dma((N,)), dma((N,)), dma(()),
        ],
        compiler_params=pltpu.CompilerParams(
            collective_id=0, has_side_effects=True, vmem_limit_bytes=60 * 1024 * 1024
        ),
    )(tokens, gate_codes, gate_scale, up_codes, up_scale, gate_keep, down_codes, down_scale.T, down_keep.T)


def solution(mesh):
    placed = (
        P("col", "row"),
        P("row", "col"),
        P("row", "col"),
        P("row", "col"),
        P("row", "col"),
        P("row", "col"),
        P("col", "row"),
        P("col", "row"),
        P("col", "row"),
    )
    return jax.shard_map(
        per_device, mesh=mesh, in_specs=placed, out_specs=P("col", "row"), check_vma=False
    )
```
